32 devices in a mesh: groups: 2 (over y), dp: 4 (over z), tensor: 2 (over x), sub: 2 (over core).
Axes of the slice: x: 2, y: 2, z: 4, core: 2. Of those that a mesh axis runs over, the one named last changes fastest.
Arguments:
- val_hidden: bfloat16 [1024, 7168], P(('groups', 'dp', 'sub'), 'tensor'), parts along dimension 0, may hold values from -6 to 6
- val_cotan: bfloat16 [1024, 4096], P(('groups', 'dp', 'sub')), parts along dimension 0, may hold values from -6 to 6
- val_count: int32 [16], P(('groups', 'dp', 'sub')), parts along dimension 0, may hold values from 16 to 64, as said below
- train_hidden: bfloat16 [2048, 7168], P(('groups', 'dp', 'sub'), 'tensor'), parts along dimension 0, may hold values from -6 to 6
- train_cotan: bfloat16 [2048, 4096], P(('groups', 'dp', 'sub')), parts along dimension 0, may hold values from -6 to 6
- seq_len: int32 [32], P('groups'), parts along dimension 0, may hold values from 1 to 64, as said below
- seq_device: int32 [32], P('groups'), parts along dimension 0, may hold values from 0 to 7, as said below
Outputs:
- weighted_grad: bfloat16 [14336, 4096], P(('groups', 'tensor'), ('dp', 'sub')), parts along dimension 0
- seq_weight: float32 [32], P('groups'), parts along dimension 0
The draws below stay inside these ranges and needn't reach their ends.
There are 2 independent parts, one for each index of `groups`. The reference program is written for one: setup_inputs(seed, part) draws one part's arguments, and reference() takes and returns one part's arrays. A program takes and returns all parts, laid end to end along the dimension named above; each array names one. Nothing has to cross between parts.
Inputs may be any that keep to these rules, and one draw needn't show every extreme that they name: `val_count`: the first data device has 16 live slots and the last data device has all 64 slots live. `seq_len`: the sequences of one device fill at most 128 slots; some device holds 2 sequences of length 64. `seq_device`: every data device holds exactly 2 sequences.
All inputs are finite; a program needn't handle non-finite values.
Results may differ from the reference program's by a relative error of at most 0.0046.
The reference program's roundings to bfloat16 on the way (of `val_kept`, `val_grad` and `weighted_cotan`) count: a program that leaves them out, or rounds other values in their place, can miss the bound.
Values may be sent and summed in bfloat16 or wider, within the bound.
A program may use at most 64 MiB of HBM per device.

```python
import jax
import jax.numpy as jnp
from jax import lax

D = 4096
FF = 7168
TOK_DEV = 128
VAL_DEV = 64
SEQ_DEV = 2
NDATA = 8
SEQS = 16
TRAIN = 1024
VAL = 512


def plan_sequences(key):
    shuffled = jax.random.permutation(jax.random.fold_in(key, 11), SEQS)
    device = (shuffled // SEQ_DEV).astype(jnp.int32)
    half_cap = TOK_DEV // SEQ_DEV
    first_draw = jax.random.randint(jax.random.fold_in(key, 12), (SEQS,), 0, half_cap + 1)
    second_draw = jax.random.randint(jax.random.fold_in(key, 13), (SEQS,), 0, half_cap + 1)
    length = jnp.maximum(first_draw * second_draw // half_cap, 1)
    full_device = jax.random.randint(jax.random.fold_in(key, 14), (), 0, NDATA)
    length = jnp.where(device == full_device, half_cap, length)
    return (length.astype(jnp.int32), device)


def draw_seq_len(key, part):
    return plan_sequences(key)[0]


def draw_seq_device(key, part):
    return plan_sequences(key)[1]


def draw_val_count(key, part):
    position = jnp.arange(NDATA, dtype=jnp.int32)
    lowest = VAL_DEV // 4
    base_count = lowest + (VAL_DEV - lowest) * position // max(NDATA - 1, 1)
    spread = max(VAL_DEV // 4, 1)
    jitter = jax.random.randint(jax.random.fold_in(key, 21), (NDATA,), -spread, spread + 1)
    counts = jnp.clip(base_count + jitter, lowest, VAL_DEV)
    counts = jnp.where(position == 0, lowest, counts)
    counts = jnp.where(position == NDATA - 1, VAL_DEV, counts)
    return counts.astype(jnp.int32)


def levels(own_key, extent, cuts, smallest, high):
    factor_of, own = 1.0, jax.random.fold_in(own_key, 6)
    for axis_at, shards_of in cuts:
        steps = jnp.exp(jax.random.uniform(jax.random.fold_in(own, axis_at), (shards_of,), jnp.float32, smallest / len(cuts), high / len(cuts)))
        factor_of = factor_of * jnp.repeat(steps, extent[axis_at] // shards_of).reshape([-1 if axis == axis_at else 1 for axis in range(len(extent))])
    return factor_of


def noise(own_key, shape, scale, most, pieces=(), kind=jnp.bfloat16):
    entries = jax.random.normal(own_key, shape, jnp.float32) * scale
    if len(pieces) > 0:
        entries = levels(own_key, shape, pieces, -0.22, 0.18) * entries
    return jnp.clip(entries, min=-most, max=most).astype(kind)


def setup_inputs(seed: int = 0, part: int = 0) -> dict:
    keys = jax.random.split(jax.random.key(seed), 8)
    own_keys = jax.random.split(jax.random.fold_in(keys[7], part), 8)
    val_hidden = noise(own_keys[0], (VAL, FF), 1.0, 6.0, ((0, 8), (1, 2)))
    val_cotan = noise(own_keys[1], (VAL, D), 1.0, 6.0, ((0, 8),))
    val_count = draw_val_count(jax.random.fold_in(jax.random.fold_in(keys[7], part), 71), part)
    train_hidden = noise(own_keys[3], (TRAIN, FF), 1.0, 6.0, ((0, 8), (1, 2)))
    train_cotan = noise(own_keys[4], (TRAIN, D), 1.0, 6.0, ((0, 8),))
    seq_len = draw_seq_len(jax.random.fold_in(jax.random.fold_in(keys[7], part), 71), part)
    seq_device = draw_seq_device(jax.random.fold_in(jax.random.fold_in(keys[7], part), 71), part)
    return {"val_hidden": val_hidden, "val_cotan": val_cotan, "val_count": val_count, "train_hidden": train_hidden, "train_cotan": train_cotan, "seq_len": seq_len, "seq_device": seq_device}


def membership(seq_len, seq_device, row_count, capacity):
    seq_order = jnp.arange(seq_len.shape[0], dtype=jnp.int32)
    shared = seq_device[:, None] == seq_device[None, :]
    earlier = seq_order[None, :] < seq_order[:, None]
    offset = lax.optimization_barrier(jnp.sum(jnp.where(shared & earlier, seq_len[None, :], 0), axis=1)).astype(jnp.int32)
    row_ids = jnp.arange(row_count, dtype=jnp.int32)
    holder = row_ids // capacity
    within = row_ids % capacity
    inside = (seq_device[None, :] == holder[:, None]) & (within[:, None] >= offset[None, :]) & (within[:, None] < (offset + seq_len)[None, :])
    return inside.astype(jnp.float32)

def reference(val_hidden, val_cotan, val_count, train_hidden, train_cotan, seq_len, seq_device):
    val_rows = jnp.arange(VAL, dtype=jnp.int32)
    val_live = val_rows % VAL_DEV < val_count[val_rows // VAL_DEV]
    val_kept = jnp.where(val_live[:, None], val_hidden, jnp.zeros_like(val_hidden))
    val_grad = jnp.dot(val_kept.T, val_cotan, preferred_element_type=jnp.float32).astype(jnp.bfloat16)
    val_total = jnp.sum(val_count).astype(jnp.float32)
    member = membership(seq_len, seq_device, TRAIN, TOK_DEV)
    projected = jnp.dot(train_hidden, val_grad, preferred_element_type=jnp.float32)
    token_align = lax.optimization_barrier(jnp.sum(projected * train_cotan.astype(jnp.float32), axis=1))
    align = jnp.dot(token_align, member, precision=lax.Precision.HIGHEST)
    lengths = seq_len.astype(jnp.float32)
    score = align / jnp.sqrt(val_total * lengths * float(FF) * float(D))
    seq_weight = jax.nn.sigmoid(score)
    mass = jnp.sum(seq_weight * lengths)
    row_weight = jnp.dot(member, seq_weight, precision=lax.Precision.HIGHEST)
    weighted_cotan = (row_weight[:, None] * train_cotan.astype(jnp.float32)).astype(jnp.bfloat16)
    weighted = jnp.dot(train_hidden.T, weighted_cotan, preferred_element_type=jnp.float32) / jnp.sqrt(mass)
    return (weighted.astype(jnp.bfloat16), seq_weight)
```

```python
import functools

import jax
import jax.numpy as jnp
from jax import lax
from jax.experimental import pallas as pl
from jax.experimental.pallas import tpu as pltpu
from jax.sharding import PartitionSpec as P

D = 4096
FF = 7168
LANES = 128
F32 = jnp.float32
BF16 = jnp.bfloat16
PIECES = 7


def membership(seq_len, seq_device, row_count, capacity):
    seq_order = jnp.arange(seq_len.shape[0], dtype=jnp.int32)
    shared = seq_device[:, None] == seq_device[None, :]
    earlier = seq_order[None, :] < seq_order[:, None]
    offset = jnp.sum(jnp.where(shared & earlier, seq_len[None, :], 0), axis=1)
    row_ids = jnp.arange(row_count, dtype=jnp.int32)
    holder = row_ids // capacity
    within = row_ids % capacity
    inside = (
        (seq_device[None, :] == holder[:, None])
        & (within[:, None] >= offset[None, :])
        & (within[:, None] < (offset + seq_len)[None, :])
    )
    return inside.astype(F32)


def kernel(
    nz, nx, hv_ref, cv_ref, count_ref, h_ref, c_ref, member_ref, len_ref,
    out_ref, weight_ref,
    h_all, hv_all, c_all, cv_all, grad, turned, weighted, acc, near, across, along,
    h_right, h_left, h_recv, h_give, h_get,
    hv_right, hv_left, hv_recv, hv_give, hv_get,
    c_send, c_recv, cv_send, cv_recv,
    near_send, near_recv, across_send, across_recv, along_send, along_recv,
):
    z = lax.axis_index("dp")
    x = lax.axis_index("tensor")
    s = lax.axis_index("sub")
    mate = 1 - s
    span = c_all.shape[3]
    toks, width = h_ref.shape
    vals = hv_ref.shape[0]

    barrier = pltpu.get_barrier_semaphore()
    for step in range(1, 2 * nz):
        other = lax.rem(z * 2 + s + step, 2 * nz)
        pl.semaphore_signal(barrier, inc=1, device_id={"dp": other // 2, "sub": lax.rem(other, 2)})
    for step in range(1, nx):
        pl.semaphore_signal(barrier, inc=1, device_id={"tensor": lax.rem(x + step, nx)})

    live = lax.broadcasted_iota(jnp.int32, hv_ref.shape, 0) < count_ref[0]
    hv_all[z, s] = jnp.where(live, hv_ref[...], jnp.zeros_like(hv_ref))
    h_all[z, s] = h_ref[...]
    pl.semaphore_wait(barrier, 2 * nz - 1 + nx - 1)

    def hop(full, b, k, rows, send, recv, target):
        ref = full.at[b, s, pl.ds(k * rows, rows)]
        return pltpu.make_async_remote_copy(
            src_ref=ref, dst_ref=ref, send_sem=send.at[b, k], recv_sem=recv.at[b, k],
            device_id=target,
        )

    class Line:
        def __init__(self, full, pieces, right, left, recv, give, get):
            self.full, self.pieces = full, pieces
            self.rows = full.shape[2] // pieces
            self.right_sem, self.left_sem, self.recv = right, left, recv
            self.give_sem, self.get = give, get

        def right(self, b, k):
            return hop(self.full, b, k, self.rows, self.right_sem, self.recv, {"dp": jnp.minimum(z + 1, nz - 1)})

        def left(self, b, k):
            return hop(self.full, b, k, self.rows, self.left_sem, self.recv, {"dp": jnp.maximum(z - 1, 0)})

        def give(self, b, k):
            return hop(self.full, b, k, self.rows, self.give_sem, self.get, {"sub": mate})

        def landed(self, b, k):
            self.right(b, k).wait_recv()

        def got(self, b):
            for k in range(self.pieces):
                self.give(b, k).wait_recv()

        def begin(self):
            for k in range(self.pieces):
                @pl.when(z < nz - 1)
                def _():
                    self.right(z, k).start()

                @pl.when(z > 0)
                def _():
                    self.left(z, k).start()

            for k in range(self.pieces):
                self.give(z, k).start()

        def relay(self, t):
            for k in range(self.pieces):
                @pl.when(z - t >= 0)
                def _():
                    b = z - t
                    self.landed(b, k)

                    @pl.when(z < nz - 1)
                    def _():
                        self.right(b, k).start()

                    self.give(b, k).start()

                @pl.when(z + t < nz)
                def _():
                    b = z + t
                    self.landed(b, k)

                    @pl.when(z > 0)
                    def _():
                        self.left(b, k).start()

                    self.give(b, k).start()

        def finish(self):
            def body(b, carry):
                for k in range(self.pieces):
                    self.give(b, k).wait_send()

                    @pl.when((b <= z) & (z < nz - 1))
                    def _():
                        self.right(b, k).wait_send()

                    @pl.when((b >= z) & (z > 0))
                    def _():
                        self.left(b, k).wait_send()

                return carry

            lax.fori_loop(0, nz, body, 0)

    hv_line = Line(hv_all, hv_right.shape[1], hv_right, hv_left, hv_recv, hv_give, hv_get)
    h_line = Line(h_all, h_right.shape[1], h_right, h_left, h_recv, h_give, h_get)

    def columns(src, full, send, recv, step):
        other = lax.rem(z * 2 + s + step, 2 * nz)
        return pltpu.make_async_remote_copy(
            src_ref=src.at[:, pl.ds(pl.multiple_of(other * span, span), span)],
            dst_ref=full.at[z, s],
            send_sem=send.at[step - 1], recv_sem=recv.at[step - 1],
            device_id={"dp": other // 2, "sub": lax.rem(other, 2)},
        )

    def each_column(do):
        def body(step, carry):
            do(step)
            return carry

        lax.fori_loop(1, 2 * nz, body, 0)

    def start_cv(step):
        columns(cv_ref, cv_all, cv_send, cv_recv, step).start()

    def start_c(step):
        columns(c_ref, c_all, c_send, c_recv, step).start()

    own = pl.ds(pl.multiple_of((z * 2 + s) * span, span), span)
    hv_line.begin()
    each_column(start_cv)
    h_line.begin()
    each_column(start_c)
    cv_all[z, s] = cv_ref[:, own]
    c_all[z, s] = c_ref[:, own]
    acc[...] = jnp.zeros_like(acc)

    def hv_step(t, carry):
        hv_line.relay(t)
        return carry

    lax.fori_loop(1, nz, hv_step, 0)
    each_column(lambda step: columns(cv_ref, cv_all, cv_send, cv_recv, step).wait())

    def hv_mate(b, carry):
        hv_line.got(b)
        return carry

    lax.fori_loop(0, nz, hv_mate, 0)

    piece = width // PIECES
    cv_flat = cv_all[...].reshape(2 * nz * vals, span)

    def grad_piece(i, carry):
        at = pl.ds(pl.multiple_of(i * piece, LANES), piece)
        left = hv_all[:, :, :, at].reshape(2 * nz * vals, piece)
        grad[at, :] = lax.dot_general(
            left, cv_flat, (((0,), (0,)), ((), ())), preferred_element_type=F32
        ).astype(BF16)
        return carry

    lax.fori_loop(0, PIECES, grad_piece, 0)
    each_column(lambda step: columns(c_ref, c_all, c_send, c_recv, step).wait())

    def use(b, core):
        block = h_all[b, core]
        projected = jnp.dot(block, grad[...], preferred_element_type=F32)
        token = jnp.sum(projected * c_all[b, core].astype(F32), axis=1, keepdims=True)
        acc[0:1, :] += jnp.sum(token * member_ref[b, core], axis=0, keepdims=True)
        spot = pl.ds(pl.multiple_of((b * 2 + core) * toks, LANES), toks)

        def turn(i, carry):
            at = pl.ds(pl.multiple_of(i * piece, LANES), piece)
            turned[at, spot] = h_all[b, core, :, at].T
            return carry

        lax.fori_loop(0, PIECES, turn, 0)

    use(z, s)
    h_line.got(z)
    use(z, mate)

    def both(b):
        use(b, s)
        h_line.got(b)
        use(b, mate)

    def h_step(t, carry):
        h_line.relay(t)

        @pl.when(z - t >= 0)
        def _():
            both(z - t)

        @pl.when(z + t < nz)
        def _():
            both(z + t)

        return carry

    lax.fori_loop(1, nz, h_step, 0)

    row = lax.broadcasted_iota(jnp.int32, acc.shape, 0)
    counted = jnp.where(row == 1, count_ref[0].astype(F32), acc[...])

    def exchange(value, buf, here, n, axis, send, recv):
        buf[here] = value
        copies = []
        for step in range(1, n):
            copy = pltpu.make_async_remote_copy(
                src_ref=buf.at[here], dst_ref=buf.at[here],
                send_sem=send.at[step - 1], recv_sem=recv.at[step - 1],
                device_id={axis: lax.rem(here + step, n)},
            )
            copy.start()
            copies.append(copy)
        for copy in copies:
            copy.wait()
        total = buf[0]
        for i in range(1, n):
            total = total + buf[i]
        return total

    total = exchange(counted, near, s, 2, "sub", near_send, near_recv)
    if nx > 1:
        total = exchange(total, across, x, nx, "tensor", across_send, across_recv)
    total = exchange(total, along, z, nz, "dp", along_send, along_recv)
    align = total[0:1, :]
    val_total = total[1:2, :] / float(nx)
    lengths = len_ref[...]
    score = align / jnp.sqrt(val_total * jnp.maximum(lengths, 1.0) * float(FF) * float(D))
    weight = 1.0 / (1.0 + jnp.exp(-score))
    weight_ref[...] = weight
    mass = jnp.sum(weight * lengths, axis=1, keepdims=True)
    root = jnp.sqrt(mass)

    def weigh(b, carry):
        for core in range(2):
            each = jnp.sum(member_ref[b, core] * weight, axis=1, keepdims=True)
            spot = pl.ds(pl.multiple_of((b * 2 + core) * toks, LANES), toks)
            weighted[spot, :] = (each * c_all[b, core].astype(F32)).astype(BF16)
        return carry

    lax.fori_loop(0, nz, weigh, 0)

    def final(i, carry):
        at = pl.ds(pl.multiple_of(i * piece, LANES), piece)
        product = jnp.dot(turned[at, :], weighted[...], preferred_element_type=F32)
        out_ref[at, :] = (product / root).astype(BF16)
        return carry

    lax.fori_loop(0, PIECES, final, 0)
    hv_line.finish()
    h_line.finish()


def shards(nz, nx, val_hidden, val_cotan, val_count, train_hidden, train_cotan, seq_len, seq_device):
    vals, width = val_hidden.shape
    toks = train_hidden.shape[0]
    span = D // (2 * nz)
    seqs = seq_len.shape[0]
    member = membership(seq_len, seq_device, 2 * nz * toks, toks)
    member = jnp.pad(member, ((0, 0), (0, LANES - seqs))).reshape(nz, 2, toks, LANES)
    lengths = jnp.pad(seq_len.astype(F32), (0, LANES - seqs)).reshape(1, LANES)
    sem = lambda *shape: pltpu.SemaphoreType.DMA(shape)
    hp, vp = (4, 2) if nz <= 4 else (1, 1)
    vmem = pl.BlockSpec(memory_space=pltpu.VMEM)
    smem = pl.BlockSpec(memory_space=pltpu.SMEM)
    out, weight = pl.pallas_call(
        functools.partial(kernel, nz, nx),
        out_shape=(
            jax.ShapeDtypeStruct((width, span), BF16),
            jax.ShapeDtypeStruct((1, LANES), F32),
        ),
        in_specs=[vmem, vmem, smem, vmem, vmem, vmem, vmem],
        out_specs=(vmem, vmem),
        scratch_shapes=[
            pltpu.VMEM((nz, 2, toks, width), BF16),
            pltpu.VMEM((nz, 2, vals, width), BF16),
            pltpu.VMEM((nz, 2, toks, span), BF16),
            pltpu.VMEM((nz, 2, vals, span), BF16),
            pltpu.VMEM((width, span), BF16),
            pltpu.VMEM((width, 2 * nz * toks), BF16),
            pltpu.VMEM((2 * nz * toks, span), BF16),
            pltpu.VMEM((8, LANES), F32),
            pltpu.VMEM((2, 8, LANES), F32),
            pltpu.VMEM((nx, 8, LANES), F32),
            pltpu.VMEM((nz, 8, LANES), F32),
            sem(nz, hp), sem(nz, hp), sem(nz, hp), sem(nz, hp), sem(nz, hp),
            sem(nz, vp), sem(nz, vp), sem(nz, vp), sem(nz, vp), sem(nz, vp),
            sem(2 * nz - 1), sem(2 * nz - 1), sem(2 * nz - 1), sem(2 * nz - 1),
            sem(1), sem(1), sem(max(nx - 1, 1)), sem(max(nx - 1, 1)), sem(nz - 1), sem(nz - 1),
        ],
        compiler_params=pltpu.CompilerParams(
            collective_id=0, has_side_effects=True, vmem_limit_bytes=56 * 1024 * 1024
        ),
        cost_estimate=pl.CostEstimate(flops=9400000000, bytes_accessed=20000000, transcendentals=0),
    )(val_hidden, val_cotan, val_count, train_hidden, train_cotan, member, lengths)
    return out, weight[0, :seqs]


def solution(mesh):
    return jax.shard_map(
        functools.partial(shards, mesh.shape["dp"], mesh.shape["tensor"]),
        mesh=mesh,
        in_specs=(
            P(("groups", "dp", "sub"), "tensor"),
            P(("groups", "dp", "sub"), None),
            P(("groups", "dp", "sub")),
            P(("groups", "dp", "sub"), "tensor"),
            P(("groups", "dp", "sub"), None),
            P("groups"),
            P("groups"),
        ),
        out_specs=(P(("groups", "tensor"), ("dp", "sub")), P("groups")),
        check_vma=False,
    )
```

```python
import functools

import jax
import jax.numpy as jnp
from jax import lax
from jax.experimental import pallas as pl
from jax.experimental.pallas import tpu as pltpu
from jax.sharding import PartitionSpec as P

D = 4096
FF = 7168
LANES = 128
F32 = jnp.float32
BF16 = jnp.bfloat16
PIECES = 7


def kernel(
    nz, nx, hv_ref, cv_ref, count_ref, h_ref, c_ref, len_ref, dev_ref,
    out_ref, weight_ref,
    h_all, cv_all, c_all, kept, turned, weighted, k1_all, k2_out, k2_all, near, across, along,
    h_right, h_left, h_recv, h_give, h_get,
    cv_right, cv_left, cv_recv, cv_give, cv_get,
    c_send, c_recv, c_swap, c_swapped, k2_send, k2_recv, k2_swap, k2_swapped,
    near_send, near_recv, across_send, across_recv, along_send, along_recv,
):
    z = lax.axis_index("dp")
    x = lax.axis_index("tensor")
    s = lax.axis_index("sub")
    mate = 1 - s
    span = c_all.shape[3]
    toks, width = h_ref.shape
    vals = hv_ref.shape[0]
    planes, _, _, rows_v, _ = k2_all.shape
    plane = x if planes > 1 else 0
    rows_c = toks // nx
    seqs = len_ref.shape[0]

    barrier = pltpu.get_barrier_semaphore()
    for step in range(1, 2 * nz):
        other = lax.rem(z * 2 + s + step, 2 * nz)
        pl.semaphore_signal(barrier, inc=1, device_id={"dp": other // 2, "sub": lax.rem(other, 2)})
    for step in range(1, nx):
        pl.semaphore_signal(barrier, inc=1, device_id={"tensor": lax.rem(x + step, nx)})

    cv_all[z, s] = cv_ref[pl.ds(pl.multiple_of(plane * rows_v, 16), rows_v), :]
    h_all[z, s] = h_ref[...]
    pl.semaphore_wait(barrier, 2 * nz - 1 + nx - 1)

    def hop(full, b, k, rows, send, recv, target):
        ref = full.at[b, s, pl.ds(k * rows, rows)]
        return pltpu.make_async_remote_copy(
            src_ref=ref, dst_ref=ref, send_sem=send.at[b, k], recv_sem=recv.at[b, k],
            device_id=target,
        )

    class Line:
        def __init__(self, full, pieces, right, left, recv, give, get):
            self.full, self.pieces = full, pieces
            self.rows = full.shape[2] // pieces
            self.right_sem, self.left_sem, self.recv = right, left, recv
            self.give_sem, self.get = give, get

        def right(self, b, k):
            return hop(self.full, b, k, self.rows, self.right_sem, self.recv, {"dp": jnp.minimum(z + 1, nz - 1)})

        def left(self, b, k):
            return hop(self.full, b, k, self.rows, self.left_sem, self.recv, {"dp": jnp.maximum(z - 1, 0)})

        def give(self, b, k):
            return hop(self.full, b, k, self.rows, self.give_sem, self.get, {"sub": mate})

        def landed(self, b, k):
            self.right(b, k).wait_recv()

        def got(self, b):
            for k in range(self.pieces):
                self.give(b, k).wait_recv()

        def begin(self):
            for k in range(self.pieces):
                @pl.when(z < nz - 1)
                def _():
                    self.right(z, k).start()

                @pl.when(z > 0)
                def _():
                    self.left(z, k).start()

            for k in range(self.pieces):
                self.give(z, k).start()

        def relay(self, t):
            for k in range(self.pieces):
                @pl.when(z - t >= 0)
                def _():
                    b = z - t
                    self.landed(b, k)

                    @pl.when(z < nz - 1)
                    def _():
                        self.right(b, k).start()

                    self.give(b, k).start()

                @pl.when(z + t < nz)
                def _():
                    b = z + t
                    self.landed(b, k)

                    @pl.when(z > 0)
                    def _():
                        self.left(b, k).start()

                    self.give(b, k).start()

        def finish(self):
            def body(b, carry):
                for k in range(self.pieces):
                    self.give(b, k).wait_send()

                    @pl.when((b <= z) & (z < nz - 1))
                    def _():
                        self.right(b, k).wait_send()

                    @pl.when((b >= z) & (z > 0))
                    def _():
                        self.left(b, k).wait_send()

                return carry

            lax.fori_loop(0, nz, body, 0)

    cv_line = Line(cv_all, cv_right.shape[1], cv_right, cv_left, cv_recv, cv_give, cv_get)
    h_line = Line(h_all, h_right.shape[1], h_right, h_left, h_recv, h_give, h_get)

    def others(do):
        def body(step, carry):
            other = lax.rem(z * 2 + s + step, 2 * nz)
            do(step, other // 2, lax.rem(other, 2))
            return carry

        lax.fori_loop(1, 2 * nz, body, 0)

    part = pl.ds(pl.multiple_of(x * rows_c, 16), rows_c)

    def columns(step, b, core):
        return pltpu.make_async_remote_copy(
            src_ref=c_ref.at[part, pl.ds(pl.multiple_of((b * 2 + core) * span, span), span)],
            dst_ref=c_all.at[z, s, part],
            send_sem=c_send.at[step - 1], recv_sem=c_recv.at[step - 1],
            device_id={"dp": b, "sub": core},
        )

    def products(step, b, core):
        return pltpu.make_async_remote_copy(
            src_ref=k2_out.at[b, core], dst_ref=k2_all.at[plane, z, s],
            send_sem=k2_send.at[step - 1], recv_sem=k2_recv.at[step - 1],
            device_id={"dp": b, "sub": core},
        )

    def swaps():
        copies = []
        for step in range(1, nx):
            peer = {"tensor": lax.rem(x + step, nx)}
            copies.append(pltpu.make_async_remote_copy(
                src_ref=c_all.at[:, :, part], dst_ref=c_all.at[:, :, part],
                send_sem=c_swap.at[step - 1], recv_sem=c_swapped.at[step - 1], device_id=peer,
            ))
            if planes > 1:
                copies.append(pltpu.make_async_remote_copy(
                    src_ref=k2_all.at[plane], dst_ref=k2_all.at[plane],
                    send_sem=k2_swap.at[step - 1], recv_sem=k2_swapped.at[step - 1], device_id=peer,
                ))
        return copies

    cv_line.begin()
    h_line.begin()
    others(lambda *at: columns(*at).start())
    own = pl.ds(pl.multiple_of((z * 2 + s) * span, span), span)
    c_all[z, s, part] = c_ref[part, own]
    live = lax.broadcasted_iota(jnp.int32, hv_ref.shape, 0) < count_ref[0]
    kept[...] = jnp.where(live, hv_ref[...], jnp.zeros_like(hv_ref))

    lane = lax.broadcasted_iota(jnp.int32, (1, LANES), 1)

    def lay(j, rows):
        lens, devs = rows
        return jnp.where(lane == j, len_ref[j], lens), jnp.where(lane == j, dev_ref[j], devs)

    lens, devs = lax.fori_loop(0, seqs, lay, (jnp.zeros_like(lane), jnp.full_like(lane, -1)))

    def place(j, offset):
        return offset + jnp.where((devs == dev_ref[j]) & (lane > j), len_ref[j], 0)

    offset = lax.fori_loop(0, seqs, place, jnp.zeros_like(lane))

    def member(b, core):
        within = lax.broadcasted_iota(jnp.int32, (toks, LANES), 0)
        inside = (devs == b * 2 + core) & (within >= offset) & (within < offset + lens)
        return inside.astype(F32)

    def cv_step(t, carry):
        cv_line.relay(t)
        return carry

    lax.fori_loop(1, nz, cv_step, 0)

    def multiply(b, carry):
        cv_line.got(b)
        for core in range(2):
            k2_out[b, core] = lax.dot_general(
                cv_all[b, core], c_ref[...], (((1,), (1,)), ((), ())), preferred_element_type=F32
            )
        return carry

    lax.fori_loop(0, nz, multiply, 0)
    others(lambda *at: products(*at).start())
    k2_all[plane, z, s] = k2_out[z, s]

    piece = width // PIECES

    def use(b, core):
        k1_all[b, core] = lax.dot_general(
            kept[...], h_all[b, core], (((1,), (1,)), ((), ())), preferred_element_type=F32
        )
        spot = pl.ds(pl.multiple_of((b * 2 + core) * toks, LANES), toks)

        def turn(i, carry):
            at = pl.ds(pl.multiple_of(i * piece, LANES), piece)
            turned[at, spot] = h_all[b, core, :, at].T
            return carry

        lax.fori_loop(0, PIECES, turn, 0)

    use(z, s)
    h_line.got(z)
    use(z, mate)

    def both(b):
        use(b, s)
        h_line.got(b)
        use(b, mate)

    def h_step(t, carry):
        @pl.when(t == nz - 1)
        def _():
            others(lambda *at: products(*at).wait())
            others(lambda *at: columns(*at).wait())
            for copy in swaps():
                copy.start()

        h_line.relay(t)

        @pl.when(z - t >= 0)
        def _():
            both(z - t)

        @pl.when(z + t < nz)
        def _():
            both(z + t)

        return carry

    lax.fori_loop(1, nz, h_step, 0)
    for copy in swaps():
        copy.wait()

    def align_block(b, total):
        for core in range(2):
            product = jnp.zeros((8, toks), F32)
            for i in range(planes):
                both_k = k1_all[b, core, i * rows_v : (i + 1) * rows_v] * k2_all[i, b, core]
                product = product + jnp.sum(both_k.reshape(rows_v // 8, 8, toks), axis=0)
            token = jnp.sum(product.T, axis=1, keepdims=True)
            total = total + jnp.sum(token * member(b, core), axis=0, keepdims=True)
        return total

    acc = lax.fori_loop(0, nz, align_block, jnp.zeros((1, LANES), F32))

    row = lax.broadcasted_iota(jnp.int32, (8, LANES), 0)
    counted = jnp.where(row == 1, count_ref[0].astype(F32), acc)

    def exchange(value, buf, here, n, axis, send, recv):
        buf[here] = value
        copies = []
        for step in range(1, n):
            copy = pltpu.make_async_remote_copy(
                src_ref=buf.at[here], dst_ref=buf.at[here],
                send_sem=send.at[step - 1], recv_sem=recv.at[step - 1],
                device_id={axis: lax.rem(here + step, n)},
            )
            copy.start()
            copies.append(copy)
        for copy in copies:
            copy.wait()
        total = buf[0]
        for i in range(1, n):
            total = total + buf[i]
        return total

    total = exchange(counted, near, s, 2, "sub", near_send, near_recv)
    if nx > 1:
        total = exchange(total, across, x, nx, "tensor", across_send, across_recv)
    total = exchange(total, along, z, nz, "dp", along_send, along_recv)
    align = total[0:1, :]
    val_total = total[1:2, :] / float(nx)
    lengths = lens.astype(F32)
    score = align / jnp.sqrt(val_total * jnp.maximum(lengths, 1.0) * float(FF) * float(D))
    weight = 1.0 / (1.0 + jnp.exp(-score))
    weight_ref[...] = weight[:, :seqs]
    mass = jnp.sum(weight * lengths, axis=1, keepdims=True)
    root = jnp.sqrt(mass)

    def weigh(b, carry):
        for core in range(2):
            each = jnp.sum(member(b, core) * weight, axis=1, keepdims=True)
            spot = pl.ds(pl.multiple_of((b * 2 + core) * toks, LANES), toks)
            weighted[spot, :] = (each * c_all[b, core].astype(F32)).astype(BF16)
        return carry

    lax.fori_loop(0, nz, weigh, 0)

    def final(i, carry):
        at = pl.ds(pl.multiple_of(i * piece, LANES), piece)
        product = jnp.dot(turned[at, :], weighted[...], preferred_element_type=F32)
        out_ref[at, :] = (product / root).astype(BF16)
        return carry

    lax.fori_loop(0, PIECES, final, 0)
    cv_line.finish()
    h_line.finish()


def shards(nz, nx, val_hidden, val_cotan, val_count, train_hidden, train_cotan, seq_len, seq_device):
    vals, width = val_hidden.shape
    toks = train_hidden.shape[0]
    span = D // (2 * nz)
    seqs = seq_len.shape[0]
    planes = nx if vals % (16 * nx) == 0 else 1
    rows_v = vals // planes
    sem = lambda *shape: pltpu.SemaphoreType.DMA(shape)
    hp, vp = (4, 2) if nz <= 4 else (1, 1)
    vmem = pl.BlockSpec(memory_space=pltpu.VMEM)
    smem = pl.BlockSpec(memory_space=pltpu.SMEM)
    out, weight = pl.pallas_call(
        functools.partial(kernel, nz, nx),
        out_shape=(
            jax.ShapeDtypeStruct((width, span), BF16),
            jax.ShapeDtypeStruct((1, seqs), F32),
        ),
        in_specs=[vmem, vmem, smem, vmem, vmem, smem, smem],
        out_specs=(vmem, vmem),
        scratch_shapes=[
            pltpu.VMEM((nz, 2, toks, width), BF16),
            pltpu.VMEM((nz, 2, rows_v, D), BF16),
            pltpu.VMEM((nz, 2, toks, span), BF16),
            pltpu.VMEM((vals, width), BF16),
            pltpu.VMEM((width, 2 * nz * toks), BF16),
            pltpu.VMEM((2 * nz * toks, span), BF16),
            pltpu.VMEM((nz, 2, vals, toks), F32),
            pltpu.VMEM((nz, 2, rows_v, toks), F32),
            pltpu.VMEM((planes, nz, 2, rows_v, toks), F32),
            pltpu.VMEM((2, 8, LANES), F32),
            pltpu.VMEM((nx, 8, LANES), F32),
            pltpu.VMEM((nz, 8, LANES), F32),
            sem(nz, hp), sem(nz, hp), sem(nz, hp), sem(nz, hp), sem(nz, hp),
            sem(nz, vp), sem(nz, vp), sem(nz, vp), sem(nz, vp), sem(nz, vp),
            sem(2 * nz - 1), sem(2 * nz - 1), sem(max(nx - 1, 1)), sem(max(nx - 1, 1)),
            sem(2 * nz - 1), sem(2 * nz - 1), sem(max(nx - 1, 1)), sem(max(nx - 1, 1)),
            sem(1), sem(1), sem(max(nx - 1, 1)), sem(max(nx - 1, 1)), sem(nz - 1), sem(nz - 1),
        ],
        compiler_params=pltpu.CompilerParams(
            collective_id=0, has_side_effects=True, vmem_limit_bytes=56 * 1024 * 1024
        ),
        cost_estimate=pl.CostEstimate(flops=4500000000, bytes_accessed=20000000, transcendentals=0),
    )(val_hidden, val_cotan, val_count, train_hidden, train_cotan, seq_len, seq_device)
    return out, weight.reshape(seqs)


def solution(mesh):
    return jax.shard_map(
        functools.partial(shards, mesh.shape["dp"], mesh.shape["tensor"]),
        mesh=mesh,
        in_specs=(
            P(("groups", "dp", "sub"), "tensor"),
            P(("groups", "dp", "sub"), None),
            P(("groups", "dp", "sub")),
            P(("groups", "dp", "sub"), "tensor"),
            P(("groups", "dp", "sub"), None),
            P("groups"),
            P("groups"),
        ),
        out_specs=(P(("groups", "tensor"), ("dp", "sub")), P("groups")),
        check_vma=False,
    )
```

```python
import functools

import jax
import jax.numpy as jnp
from jax import lax
from jax.experimental import pallas as pl
from jax.experimental.pallas import tpu as pltpu
from jax.sharding import PartitionSpec as P

D = 4096
FF = 7168
LANES = 128
F32 = jnp.float32
BF16 = jnp.bfloat16
PIECES = 7


def kernel(
    nz, nx, hv_ref, cv_ref, count_ref, h_ref, c_ref, len_ref, dev_ref,
    out_ref, weight_ref,
    h_all, cv_all, c_all, kept, turned, weighted, k1_all, c_far, k2_out, k2_all, near, across, along,
    h_right, h_left, h_recv, h_give, h_get,
    cv_right, cv_left, cv_recv, cv_give, cv_get,
    c_send, c_recv, c_swap, c_swapped, k2_send, k2_recv, k2_swap, k2_swapped, far_send, far_recv, far_swap, far_swapped,
    near_send, near_recv, across_send, across_recv, along_send, along_recv,
):
    z = lax.axis_index("dp")
    x = lax.axis_index("tensor")
    s = lax.axis_index("sub")
    mate = 1 - s
    span = c_all.shape[3]
    toks, width = h_ref.shape
    vals = hv_ref.shape[0]
    planes, _, _, rows_v, _ = k2_all.shape
    plane = x if planes > 1 else 0
    rows_c = toks // nx
    seqs = len_ref.shape[0]

    barrier = pltpu.get_barrier_semaphore()
    for step in range(1, 2 * nz):
        other = lax.rem(z * 2 + s + step, 2 * nz)
        pl.semaphore_signal(barrier, inc=1, device_id={"dp": other // 2, "sub": lax.rem(other, 2)})
    for step in range(1, nx):
        pl.semaphore_signal(barrier, inc=1, device_id={"tensor": lax.rem(x + step, nx)})

    cv_all[z, s] = cv_ref[pl.ds(pl.multiple_of(plane * rows_v, 16), rows_v), :]
    h_all[z, s] = h_ref[...]
    pl.semaphore_wait(barrier, 2 * nz - 1 + nx - 1)

    def hop(full, b, k, rows, send, recv, target):
        ref = full.at[b, s, pl.ds(k * rows, rows)]
        return pltpu.make_async_remote_copy(
            src_ref=ref, dst_ref=ref, send_sem=send.at[b, k], recv_sem=recv.at[b, k],
            device_id=target,
        )

    inner = (z > 0) & (z < nz - 1)
    beside = (z == 1) | (z == nz - 2)
    end = jnp.where(z == 1, 0, nz - 1)

    class Line:
        def __init__(self, skip, full, pieces, right, left, recv, give, get):
            self.sharing = inner if skip else (z >= 0)
            self.sends_right = z < nz - (2 if skip else 1)
            self.sends_left = z > (1 if skip else 0)
            self.full, self.pieces = full, pieces
            self.rows = full.shape[2] // pieces
            self.right_sem, self.left_sem, self.recv = right, left, recv
            self.give_sem, self.get = give, get

        def right(self, b, k):
            return hop(self.full, b, k, self.rows, self.right_sem, self.recv, {"dp": jnp.minimum(z + 1, nz - 1)})

        def left(self, b, k):
            return hop(self.full, b, k, self.rows, self.left_sem, self.recv, {"dp": jnp.maximum(z - 1, 0)})

        def give(self, b, k):
            return hop(self.full, b, k, self.rows, self.give_sem, self.get, {"sub": mate})

        def landed(self, b, k):
            self.right(b, k).wait_recv()

        def got(self, b):
            for k in range(self.pieces):
                self.give(b, k).wait_recv()

        def begin(self):
            for k in range(self.pieces):
                @pl.when(self.sends_right)
                def _():
                    self.right(z, k).start()

                @pl.when(self.sends_left)
                def _():
                    self.left(z, k).start()

            for k in range(self.pieces):
                @pl.when(self.sharing)
                def _():
                    self.give(z, k).start()

        def relay(self, t):
            for k in range(self.pieces):
                @pl.when((z - t >= 0) & self.sharing)
                def _():
                    b = z - t
                    self.landed(b, k)

                    @pl.when(self.sends_right)
                    def _():
                        self.right(b, k).start()

                    self.give(b, k).start()

                @pl.when((z + t < nz) & self.sharing)
                def _():
                    b = z + t
                    self.landed(b, k)

                    @pl.when(self.sends_left)
                    def _():
                        self.left(b, k).start()

                    self.give(b, k).start()

        def finish(self):
            def body(b, carry):
                for k in range(self.pieces):
                    @pl.when(self.sharing)
                    def _():
                        self.give(b, k).wait_send()

                    @pl.when((b <= z) & self.sends_right & (self.sharing | (b == z)))
                    def _():
                        self.right(b, k).wait_send()

                    @pl.when((b >= z) & self.sends_left & (self.sharing | (b == z)))
                    def _():
                        self.left(b, k).wait_send()

                return carry

            lax.fori_loop(0, nz, body, 0)

    cv_line = Line(True, cv_all, cv_right.shape[1], cv_right, cv_left, cv_recv, cv_give, cv_get)
    h_line = Line(False, h_all, h_right.shape[1], h_right, h_left, h_recv, h_give, h_get)

    def others(do):
        def body(step, carry):
            other = lax.rem(z * 2 + s + step, 2 * nz)
            do(step, other // 2, lax.rem(other, 2))
            return carry

        lax.fori_loop(1, 2 * nz, body, 0)

    part = pl.ds(pl.multiple_of(x * rows_c, 16), rows_c)

    def columns(step, b, core):
        return pltpu.make_async_remote_copy(
            src_ref=c_ref.at[part, pl.ds(pl.multiple_of((b * 2 + core) * span, span), span)],
            dst_ref=c_all.at[z, s, part],
            send_sem=c_send.at[step - 1], recv_sem=c_recv.at[step - 1],
            device_id={"dp": b, "sub": core},
        )

    def products(which, step, b, core):
        return pltpu.make_async_remote_copy(
            src_ref=k2_out.at[which, b, core], dst_ref=k2_all.at[plane, (z, end)[which], s],
            send_sem=k2_send.at[which, step - 1], recv_sem=k2_recv.at[(z, end)[which], s],
            device_id={"dp": b, "sub": core},
        )

    def product_landed(step, b, core):
        ref = k2_all.at[plane, b, core]
        pltpu.make_async_remote_copy(
            src_ref=ref, dst_ref=ref, send_sem=k2_send.at[0, 0], recv_sem=k2_recv.at[b, core],
            device_id={"sub": mate},
        ).wait_recv()

    def far():
        return pltpu.make_async_remote_copy(
            src_ref=c_ref.at[part], dst_ref=c_far.at[part], send_sem=far_send.at[0], recv_sem=far_recv.at[0],
            device_id={"dp": jnp.where(z == 0, 1, jnp.where(z == nz - 1, nz - 2, end))},
        )

    def far_swaps():
        return [
            pltpu.make_async_remote_copy(
                src_ref=c_far.at[part], dst_ref=c_far.at[part],
                send_sem=far_swap.at[step - 1], recv_sem=far_swapped.at[step - 1],
                device_id={"tensor": lax.rem(x + step, nx)},
            )
            for step in range(1, nx)
        ]

    def swaps():
        copies = []
        for step in range(1, nx):
            peer = {"tensor": lax.rem(x + step, nx)}
            copies.append(pltpu.make_async_remote_copy(
                src_ref=c_all.at[:, :, part], dst_ref=c_all.at[:, :, part],
                send_sem=c_swap.at[step - 1], recv_sem=c_swapped.at[step - 1], device_id=peer,
            ))
            if planes > 1:
                copies.append(pltpu.make_async_remote_copy(
                    src_ref=k2_all.at[plane], dst_ref=k2_all.at[plane],
                    send_sem=k2_swap.at[step - 1], recv_sem=k2_swapped.at[step - 1], device_id=peer,
                ))
        return copies

    @pl.when(jnp.logical_not(inner))
    def _():
        far().start()

    cv_line.begin()
    h_line.begin()
    others(lambda *at: columns(*at).start())
    own = pl.ds(pl.multiple_of((z * 2 + s) * span, span), span)
    c_all[z, s, part] = c_ref[part, own]
    live = lax.broadcasted_iota(jnp.int32, hv_ref.shape, 0) < count_ref[0]
    kept[...] = jnp.where(live, hv_ref[...], jnp.zeros_like(hv_ref))

    lane = lax.broadcasted_iota(jnp.int32, (1, LANES), 1)

    def lay(j, rows):
        lens, devs = rows
        return jnp.where(lane == j, len_ref[j], lens), jnp.where(lane == j, dev_ref[j], devs)

    lens, devs = lax.fori_loop(0, seqs, lay, (jnp.zeros_like(lane), jnp.full_like(lane, -1)))

    def place(j, offset):
        return offset + jnp.where((devs == dev_ref[j]) & (lane > j), len_ref[j], 0)

    offset = lax.fori_loop(0, seqs, place, jnp.zeros_like(lane))

    def member(b, core):
        within = lax.broadcasted_iota(jnp.int32, (toks, LANES), 0)
        inside = (devs == b * 2 + core) & (within >= offset) & (within < offset + lens)
        return inside.astype(F32)

    def multiply(which, c_rows):
        def body(b, carry):
            for core in range(2):
                k2_out[which, b, core] = lax.dot_general(
                    cv_all[b, core], c_rows[...], (((1,), (1,)), ((), ())), preferred_element_type=F32
                )
            return carry

        lax.fori_loop(0, nz, body, 0)
        others(lambda *at: products(which, *at).start())
        k2_all[plane, (z, end)[which], s] = k2_out[which, z, s]

    piece = width // PIECES

    def use(b, core):
        k1_all[b, core] = lax.dot_general(
            kept[...], h_all[b, core], (((1,), (1,)), ((), ())), preferred_element_type=F32
        )
        spot = pl.ds(pl.multiple_of((b * 2 + core) * toks, LANES), toks)

        def turn(i, carry):
            at = pl.ds(pl.multiple_of(i * piece, LANES), piece)
            turned[at, spot] = h_all[b, core, :, at].T
            return carry

        lax.fori_loop(0, PIECES, turn, 0)

    use(z, s)
    h_line.got(z)
    use(z, mate)

    def both(b):
        use(b, s)
        h_line.got(b)
        use(b, mate)

    def form_products():
        @pl.when(inner)
        def _():
            def got(b, carry):
                cv_line.got(b)
                return carry

            lax.fori_loop(0, nz, got, 0)
            multiply(0, c_ref)

        @pl.when(beside)
        def _():
            for copy in far_swaps():
                copy.wait()
            multiply(1, c_far)

    def h_step(t, carry):
        cv_line.relay(t)

        @pl.when(t == nz - 1)
        def _():
            def arrive(step, b, core):
                formed_here = (core == s) & beside & (b == end)

                @pl.when(jnp.logical_not(formed_here))
                def _():
                    product_landed(step, b, core)

            others(arrive)

            @pl.when(jnp.logical_not(inner))
            def _():
                product_landed(0, z, s)

            others(lambda *at: columns(*at).wait())
            for copy in swaps():
                copy.start()

        h_line.relay(t)

        @pl.when((t == 1) & beside)
        def _():
            far().wait_recv()
            for copy in far_swaps():
                copy.start()

        @pl.when(t == nz - 2)
        def _():
            form_products()

        @pl.when(z - t >= 0)
        def _():
            both(z - t)

        @pl.when(z + t < nz)
        def _():
            both(z + t)

        return carry

    lax.fori_loop(1, nz, h_step, 0)
    for copy in swaps():
        copy.wait()

    def align_block(b, total):
        for core in range(2):
            product = jnp.zeros((8, toks), F32)
            for i in range(planes):
                both_k = k1_all[b, core, i * rows_v : (i + 1) * rows_v] * k2_all[i, b, core]
                product = product + jnp.sum(both_k.reshape(rows_v // 8, 8, toks), axis=0)
            token = jnp.sum(product.T, axis=1, keepdims=True)
            total = total + jnp.sum(token * member(b, core), axis=0, keepdims=True)
        return total

    acc = lax.fori_loop(0, nz, align_block, jnp.zeros((1, LANES), F32))

    row = lax.broadcasted_iota(jnp.int32, (8, LANES), 0)
    counted = jnp.where(row == 1, count_ref[0].astype(F32), acc)

    def exchange(value, buf, here, n, axis, send, recv):
        buf[here] = value
        copies = []
        for step in range(1, n):
            copy = pltpu.make_async_remote_copy(
                src_ref=buf.at[here], dst_ref=buf.at[here],
                send_sem=send.at[step - 1], recv_sem=recv.at[step - 1],
                device_id={axis: lax.rem(here + step, n)},
            )
            copy.start()
            copies.append(copy)
        for copy in copies:
            copy.wait()
        total = buf[0]
        for i in range(1, n):
            total = total + buf[i]
        return total

    total = exchange(counted, near, s, 2, "sub", near_send, near_recv)
    if nx > 1:
        total = exchange(total, across, x, nx, "tensor", across_send, across_recv)
    total = exchange(total, along, z, nz, "dp", along_send, along_recv)
    align = total[0:1, :]
    val_total = total[1:2, :] / float(nx)
    lengths = lens.astype(F32)
    score = align / jnp.sqrt(val_total * jnp.maximum(lengths, 1.0) * float(FF) * float(D))
    weight = 1.0 / (1.0 + jnp.exp(-score))
    weight_ref[...] = weight[:, :seqs]
    mass = jnp.sum(weight * lengths, axis=1, keepdims=True)
    root = jnp.sqrt(mass)

    def weigh(b, carry):
        for core in range(2):
            each = jnp.sum(member(b, core) * weight, axis=1, keepdims=True)
            spot = pl.ds(pl.multiple_of((b * 2 + core) * toks, LANES), toks)
            weighted[spot, :] = (each * c_all[b, core].astype(F32)).astype(BF16)
        return carry

    lax.fori_loop(0, nz, weigh, 0)

    def final(i, carry):
        at = pl.ds(pl.multiple_of(i * piece, LANES), piece)
        product = jnp.dot(turned[at, :], weighted[...], preferred_element_type=F32)
        out_ref[at, :] = (product / root).astype(BF16)
        return carry

    lax.fori_loop(0, PIECES, final, 0)
    @pl.when(jnp.logical_not(inner))
    def _():
        far().wait_send()

    @pl.when(inner)
    def _():
        others(lambda *at: products(0, *at).wait_send())

    @pl.when(beside)
    def _():
        others(lambda *at: products(1, *at).wait_send())

    cv_line.finish()
    h_line.finish()


def shards(nz, nx, val_hidden, val_cotan, val_count, train_hidden, train_cotan, seq_len, seq_device):
    vals, width = val_hidden.shape
    toks = train_hidden.shape[0]
    span = D // (2 * nz)
    seqs = seq_len.shape[0]
    planes = nx if vals % (16 * nx) == 0 else 1
    rows_v = vals // planes
    sem = lambda *shape: pltpu.SemaphoreType.DMA(shape)
    hp, vp = (4, 2) if nz <= 4 else (1, 1)
    vmem = pl.BlockSpec(memory_space=pltpu.VMEM)
    smem = pl.BlockSpec(memory_space=pltpu.SMEM)
    out, weight = pl.pallas_call(
        functools.partial(kernel, nz, nx),
        out_shape=(
            jax.ShapeDtypeStruct((width, span), BF16),
            jax.ShapeDtypeStruct((1, seqs), F32),
        ),
        in_specs=[vmem, vmem, smem, vmem, vmem, smem, smem],
        out_specs=(vmem, vmem),
        scratch_shapes=[
            pltpu.VMEM((nz, 2, toks, width), BF16),
            pltpu.VMEM((nz, 2, rows_v, D), BF16),
            pltpu.VMEM((nz, 2, toks, span), BF16),
            pltpu.VMEM((vals, width), BF16),
            pltpu.VMEM((width, 2 * nz * toks), BF16),
            pltpu.VMEM((2 * nz * toks, span), BF16),
            pltpu.VMEM((nz, 2, vals, toks), F32),
            pltpu.VMEM((toks, D), BF16),
            pltpu.VMEM((2, nz, 2, rows_v, toks), F32),
            pltpu.VMEM((planes, nz, 2, rows_v, toks), F32),
            pltpu.VMEM((2, 8, LANES), F32),
            pltpu.VMEM((nx, 8, LANES), F32),
            pltpu.VMEM((nz, 8, LANES), F32),
            sem(nz, hp), sem(nz, hp), sem(nz, hp), sem(nz, hp), sem(nz, hp),
            sem(nz, vp), sem(nz, vp), sem(nz, vp), sem(nz, vp), sem(nz, vp),
            sem(2 * nz - 1), sem(2 * nz - 1), sem(max(nx - 1, 1)), sem(max(nx - 1, 1)),
            sem(2, 2 * nz - 1), sem(nz, 2), sem(max(nx - 1, 1)), sem(max(nx - 1, 1)),
            sem(1), sem(1), sem(max(nx - 1, 1)), sem(max(nx - 1, 1)),
            sem(1), sem(1), sem(max(nx - 1, 1)), sem(max(nx - 1, 1)), sem(nz - 1), sem(nz - 1),
        ],
        compiler_params=pltpu.CompilerParams(
            collective_id=0, has_side_effects=True, vmem_limit_bytes=56 * 1024 * 1024
        ),
        cost_estimate=pl.CostEstimate(flops=4500000000, bytes_accessed=20000000, transcendentals=0),
    )(val_hidden, val_cotan, val_count, train_hidden, train_cotan, seq_len, seq_device)
    return out, weight.reshape(seqs)


def solution(mesh):
    return jax.shard_map(
        functools.partial(shards, mesh.shape["dp"], mesh.shape["tensor"]),
        mesh=mesh,
        in_specs=(
            P(("groups", "dp", "sub"), "tensor"),
            P(("groups", "dp", "sub"), None),
            P(("groups", "dp", "sub")),
            P(("groups", "dp", "sub"), "tensor"),
            P(("groups", "dp", "sub"), None),
            P("groups"),
            P("groups"),
        ),
        out_specs=(P(("groups", "tensor"), ("dp", "sub")), P("groups")),
        check_vma=False,
    )
```

```python
import functools

import jax
import jax.numpy as jnp
from jax import lax
from jax.experimental import pallas as pl
from jax.experimental.pallas import tpu as pltpu
from jax.sharding import PartitionSpec as P

D = 4096
FF = 7168
LANES = 128
F32 = jnp.float32
BF16 = jnp.bfloat16
PIECES = 7


def kernel(
    nz, nx, hv_src, cv_src, count_ref, h_src, c_src, len_ref, dev_ref,
    out_hbm, weight_ref,
    out_ref, left_sem, hv_ref, c_ref, fetched,
    h_all, cv_all, c_all, kept, turned, weighted, k1_all, c_far, k2_out, k2_all, near, across, along,
    h_right, h_left, h_recv, h_give, h_get,
    cv_right, cv_left, cv_recv, cv_give, cv_get,
    c_send, c_recv, c_swap, c_swapped, k2_send, k2_recv, k2_swap, k2_swapped, far_send, far_recv, far_swap, far_swapped,
    near_send, near_recv, across_send, across_recv, along_send, along_recv,
):
    z = lax.axis_index("dp")
    x = lax.axis_index("tensor")
    s = lax.axis_index("sub")
    mate = 1 - s
    span = c_all.shape[3]
    toks, width = h_src.shape
    vals = hv_ref.shape[0]
    planes, _, _, rows_v, _ = k2_all.shape
    plane = x if planes > 1 else 0
    rows_c = toks // nx
    seqs = len_ref.shape[0]

    rows_here = pl.ds(pl.multiple_of(plane * rows_v, 16), rows_v)
    fetches = [
        pltpu.make_async_copy(cv_src.at[rows_here], cv_all.at[z, s], fetched.at[0]),
        pltpu.make_async_copy(h_src, h_all.at[z, s], fetched.at[1]),
        pltpu.make_async_copy(c_src, c_ref, fetched.at[2]),
        pltpu.make_async_copy(hv_src, hv_ref, fetched.at[3]),
    ]
    for fetch in fetches:
        fetch.start()
    barrier = pltpu.get_barrier_semaphore()
    for step in range(1, 2 * nz):
        other = lax.rem(z * 2 + s + step, 2 * nz)
        pl.semaphore_signal(barrier, inc=1, device_id={"dp": other // 2, "sub": lax.rem(other, 2)})
    for step in range(1, nx):
        pl.semaphore_signal(barrier, inc=1, device_id={"tensor": lax.rem(x + step, nx)})

    pl.semaphore_wait(barrier, 2 * nz - 1 + nx - 1)

    def hop(full, b, k, rows, send, recv, target):
        ref = full.at[b, s, pl.ds(k * rows, rows)]
        return pltpu.make_async_remote_copy(
            src_ref=ref, dst_ref=ref, send_sem=send.at[b, k], recv_sem=recv.at[b, k],
            device_id=target,
        )

    inner = (z > 0) & (z < nz - 1)
    beside = (z == 1) | (z == nz - 2)
    end = jnp.where(z == 1, 0, nz - 1)

    class Line:
        def __init__(self, skip, full, pieces, right, left, recv, give, get):
            self.sharing = inner if skip else (z >= 0)
            self.sends_right = z < nz - (2 if skip else 1)
            self.sends_left = z > (1 if skip else 0)
            self.full, self.pieces = full, pieces
            self.rows = full.shape[2] // pieces
            self.right_sem, self.left_sem, self.recv = right, left, recv
            self.give_sem, self.get = give, get

        def right(self, b, k):
            return hop(self.full, b, k, self.rows, self.right_sem, self.recv, {"dp": jnp.minimum(z + 1, nz - 1)})

        def left(self, b, k):
            return hop(self.full, b, k, self.rows, self.left_sem, self.recv, {"dp": jnp.maximum(z - 1, 0)})

        def give(self, b, k):
            return hop(self.full, b, k, self.rows, self.give_sem, self.get, {"sub": mate})

        def landed(self, b, k):
            self.right(b, k).wait_recv()

        def got(self, b):
            for k in range(self.pieces):
                self.give(b, k).wait_recv()

        def begin(self):
            for k in range(self.pieces):
                @pl.when(self.sends_right)
                def _():
                    self.right(z, k).start()

                @pl.when(self.sends_left)
                def _():
                    self.left(z, k).start()

            for k in range(self.pieces):
                @pl.when(self.sharing)
                def _():
                    self.give(z, k).start()

        def relay(self, t):
            for k in range(self.pieces):
                @pl.when((z - t >= 0) & self.sharing)
                def _():
                    b = z - t
                    self.landed(b, k)

                    @pl.when(self.sends_right)
                    def _():
                        self.right(b, k).start()

                    self.give(b, k).start()

                @pl.when((z + t < nz) & self.sharing)
                def _():
                    b = z + t
                    self.landed(b, k)

                    @pl.when(self.sends_left)
                    def _():
                        self.left(b, k).start()

                    self.give(b, k).start()

        def finish(self):
            def body(b, carry):
                for k in range(self.pieces):
                    @pl.when(self.sharing)
                    def _():
                        self.give(b, k).wait_send()

                    @pl.when((b <= z) & self.sends_right & (self.sharing | (b == z)))
                    def _():
                        self.right(b, k).wait_send()

                    @pl.when((b >= z) & self.sends_left & (self.sharing | (b == z)))
                    def _():
                        self.left(b, k).wait_send()

                return carry

            lax.fori_loop(0, nz, body, 0)

    cv_line = Line(True, cv_all, cv_right.shape[1], cv_right, cv_left, cv_recv, cv_give, cv_get)
    h_line = Line(False, h_all, h_right.shape[1], h_right, h_left, h_recv, h_give, h_get)

    def others(do):
        def body(step, carry):
            other = lax.rem(z * 2 + s + step, 2 * nz)
            do(step, other // 2, lax.rem(other, 2))
            return carry

        lax.fori_loop(1, 2 * nz, body, 0)

    part = pl.ds(pl.multiple_of(x * rows_c, 16), rows_c)

    def columns(step, b, core):
        return pltpu.make_async_remote_copy(
            src_ref=c_ref.at[part, pl.ds(pl.multiple_of((b * 2 + core) * span, span), span)],
            dst_ref=c_all.at[z, s, part],
            send_sem=c_send.at[step - 1], recv_sem=c_recv.at[step - 1],
            device_id={"dp": b, "sub": core},
        )

    def products(which, step, b, core):
        return pltpu.make_async_remote_copy(
            src_ref=k2_out.at[which, b, core], dst_ref=k2_all.at[plane, (z, end)[which], s],
            send_sem=k2_send.at[which, step - 1], recv_sem=k2_recv.at[(z, end)[which], s],
            device_id={"dp": b, "sub": core},
        )

    def product_landed(step, b, core):
        ref = k2_all.at[plane, b, core]
        pltpu.make_async_remote_copy(
            src_ref=ref, dst_ref=ref, send_sem=k2_send.at[0, 0], recv_sem=k2_recv.at[b, core],
            device_id={"sub": mate},
        ).wait_recv()

    def far():
        return pltpu.make_async_remote_copy(
            src_ref=c_ref.at[part], dst_ref=c_far.at[part], send_sem=far_send.at[0], recv_sem=far_recv.at[0],
            device_id={"dp": jnp.where(z == 0, 1, jnp.where(z == nz - 1, nz - 2, end))},
        )

    def far_swaps():
        return [
            pltpu.make_async_remote_copy(
                src_ref=c_far.at[part], dst_ref=c_far.at[part],
                send_sem=far_swap.at[step - 1], recv_sem=far_swapped.at[step - 1],
                device_id={"tensor": lax.rem(x + step, nx)},
            )
            for step in range(1, nx)
        ]

    def swaps():
        copies = []
        for step in range(1, nx):
            peer = {"tensor": lax.rem(x + step, nx)}
            copies.append(pltpu.make_async_remote_copy(
                src_ref=c_all.at[:, :, part], dst_ref=c_all.at[:, :, part],
                send_sem=c_swap.at[step - 1], recv_sem=c_swapped.at[step - 1], device_id=peer,
            ))
            if planes > 1:
                copies.append(pltpu.make_async_remote_copy(
                    src_ref=k2_all.at[plane], dst_ref=k2_all.at[plane],
                    send_sem=k2_swap.at[step - 1], recv_sem=k2_swapped.at[step - 1], device_id=peer,
                ))
        return copies

    fetches[0].wait()
    cv_line.begin()
    fetches[1].wait()
    h_line.begin()
    fetches[2].wait()

    @pl.when(jnp.logical_not(inner))
    def _():
        far().start()

    others(lambda *at: columns(*at).start())
    own = pl.ds(pl.multiple_of((z * 2 + s) * span, span), span)
    c_all[z, s, part] = c_ref[part, own]
    fetches[3].wait()
    live = lax.broadcasted_iota(jnp.int32, hv_ref.shape, 0) < count_ref[0]
    kept[...] = jnp.where(live, hv_ref[...], jnp.zeros_like(hv_ref))

    lane = lax.broadcasted_iota(jnp.int32, (1, LANES), 1)

    def lay(j, rows):
        lens, devs = rows
        return jnp.where(lane == j, len_ref[j], lens), jnp.where(lane == j, dev_ref[j], devs)

    lens, devs = lax.fori_loop(0, seqs, lay, (jnp.zeros_like(lane), jnp.full_like(lane, -1)))

    def place(j, offset):
        return offset + jnp.where((devs == dev_ref[j]) & (lane > j), len_ref[j], 0)

    offset = lax.fori_loop(0, seqs, place, jnp.zeros_like(lane))

    def member(b, core):
        within = lax.broadcasted_iota(jnp.int32, (toks, LANES), 0)
        inside = (devs == b * 2 + core) & (within >= offset) & (within < offset + lens)
        return inside.astype(F32)

    def multiply(which, c_rows):
        def body(b, carry):
            for core in range(2):
                k2_out[which, b, core] = lax.dot_general(
                    cv_all[b, core], c_rows[...], (((1,), (1,)), ((), ())), preferred_element_type=F32
                )
            return carry

        lax.fori_loop(0, nz, body, 0)
        others(lambda *at: products(which, *at).start())
        k2_all[plane, (z, end)[which], s] = k2_out[which, z, s]

    piece = width // PIECES

    def use(b, core):
        k1_all[b, core] = lax.dot_general(
            kept[...], h_all[b, core], (((1,), (1,)), ((), ())), preferred_element_type=F32
        )
        spot = pl.ds(pl.multiple_of((b * 2 + core) * toks, LANES), toks)

        def turn(i, carry):
            at = pl.ds(pl.multiple_of(i * piece, LANES), piece)
            turned[at, spot] = h_all[b, core, :, at].T
            return carry

        lax.fori_loop(0, PIECES, turn, 0)

    use(z, s)
    h_line.got(z)
    use(z, mate)

    def both(b):
        use(b, s)
        h_line.got(b)
        use(b, mate)

    def form_products():
        @pl.when(inner)
        def _():
            def got(b, carry):
                cv_line.got(b)
                return carry

            lax.fori_loop(0, nz, got, 0)
            multiply(0, c_ref)

        @pl.when(beside)
        def _():
            for copy in far_swaps():
                copy.wait()
            multiply(1, c_far)

    def h_step(t, carry):
        cv_line.relay(t)

        @pl.when(t == nz - 1)
        def _():
            def arrive(step, b, core):
                formed_here = (core == s) & beside & (b == end)

                @pl.when(jnp.logical_not(formed_here))
                def _():
                    product_landed(step, b, core)

            others(arrive)

            @pl.when(jnp.logical_not(inner))
            def _():
                product_landed(0, z, s)

            others(lambda *at: columns(*at).wait())
            for copy in swaps():
                copy.start()

        h_line.relay(t)

        @pl.when((t == 1) & beside)
        def _():
            far().wait_recv()
            for copy in far_swaps():
                copy.start()

        @pl.when(t == nz - 2)
        def _():
            form_products()

        @pl.when(z - t >= 0)
        def _():
            both(z - t)

        @pl.when(z + t < nz)
        def _():
            both(z + t)

        return carry

    lax.fori_loop(1, nz, h_step, 0)
    for copy in swaps():
        copy.wait()

    def align_block(b, total):
        for core in range(2):
            product = jnp.zeros((8, toks), F32)
            for i in range(planes):
                both_k = k1_all[b, core, i * rows_v : (i + 1) * rows_v] * k2_all[i, b, core]
                product = product + jnp.sum(both_k.reshape(rows_v // 8, 8, toks), axis=0)
            token = jnp.sum(product.T, axis=1, keepdims=True)
            total = total + jnp.sum(token * member(b, core), axis=0, keepdims=True)
        return total

    acc = lax.fori_loop(0, nz, align_block, jnp.zeros((1, LANES), F32))

    row = lax.broadcasted_iota(jnp.int32, (8, LANES), 0)
    counted = jnp.where(row == 1, count_ref[0].astype(F32), acc)

    def exchange(value, buf, here, n, axis, send, recv):
        buf[here] = value
        copies = []
        for step in range(1, n):
            copy = pltpu.make_async_remote_copy(
                src_ref=buf.at[here], dst_ref=buf.at[here],
                send_sem=send.at[step - 1], recv_sem=recv.at[step - 1],
                device_id={axis: lax.rem(here + step, n)},
            )
            copy.start()
            copies.append(copy)
        for copy in copies:
            copy.wait()
        total = buf[0]
        for i in range(1, n):
            total = total + buf[i]
        return total

    total = exchange(counted, near, s, 2, "sub", near_send, near_recv)
    if nx > 1:
        total = exchange(total, across, x, nx, "tensor", across_send, across_recv)
    total = exchange(total, along, z, nz, "dp", along_send, along_recv)
    align = total[0:1, :]
    val_total = total[1:2, :] / float(nx)
    lengths = lens.astype(F32)
    score = align / jnp.sqrt(val_total * jnp.maximum(lengths, 1.0) * float(FF) * float(D))
    weight = 1.0 / (1.0 + jnp.exp(-score))
    weight_ref[...] = weight[:, :seqs]
    mass = jnp.sum(weight * lengths, axis=1, keepdims=True)
    root = jnp.sqrt(mass)

    def weigh(b, carry):
        for core in range(2):
            each = jnp.sum(member(b, core) * weight, axis=1, keepdims=True)
            spot = pl.ds(pl.multiple_of((b * 2 + core) * toks, LANES), toks)
            weighted[spot, :] = (each * c_all[b, core].astype(F32)).astype(BF16)
        return carry

    lax.fori_loop(0, nz, weigh, 0)

    def final(i, carry):
        at = pl.ds(pl.multiple_of(i * piece, LANES), piece)
        product = jnp.dot(turned[at, :], weighted[...], preferred_element_type=F32)
        out_ref[at, :] = (product / root).astype(BF16)
        pltpu.make_async_copy(out_ref.at[at], out_hbm.at[at], left_sem.at[i]).start()
        return carry

    lax.fori_loop(0, PIECES, final, 0)

    def left(i, carry):
        at = pl.ds(pl.multiple_of(i * piece, LANES), piece)
        pltpu.make_async_copy(out_ref.at[at], out_hbm.at[at], left_sem.at[i]).wait()
        return carry

    lax.fori_loop(0, PIECES, left, 0)
    @pl.when(jnp.logical_not(inner))
    def _():
        far().wait_send()

    @pl.when(inner)
    def _():
        others(lambda *at: products(0, *at).wait_send())

    @pl.when(beside)
    def _():
        others(lambda *at: products(1, *at).wait_send())

    cv_line.finish()
    h_line.finish()


def shards(nz, nx, val_hidden, val_cotan, val_count, train_hidden, train_cotan, seq_len, seq_device):
    vals, width = val_hidden.shape
    toks = train_hidden.shape[0]
    span = D // (2 * nz)
    seqs = seq_len.shape[0]
    planes = nx if vals % (16 * nx) == 0 else 1
    rows_v = vals // planes
    sem = lambda *shape: pltpu.SemaphoreType.DMA(shape)
    hp, vp = (4, 2) if nz <= 4 else (1, 1)
    vmem = pl.BlockSpec(memory_space=pltpu.VMEM)
    hbm = pl.BlockSpec(memory_space=pl.ANY)
    smem = pl.BlockSpec(memory_space=pltpu.SMEM)
    out, weight = pl.pallas_call(
        functools.partial(kernel, nz, nx),
        out_shape=(
            jax.ShapeDtypeStruct((width, span), BF16),
            jax.ShapeDtypeStruct((1, seqs), F32),
        ),
        in_specs=[hbm, hbm, smem, hbm, hbm, smem, smem],
        out_specs=(hbm, vmem),
        scratch_shapes=[
            pltpu.VMEM((width, span), BF16), sem(PIECES),
            pltpu.VMEM((vals, width), BF16), pltpu.VMEM((toks, D), BF16), sem(4),
            pltpu.VMEM((nz, 2, toks, width), BF16),
            pltpu.VMEM((nz, 2, rows_v, D), BF16),
            pltpu.VMEM((nz, 2, toks, span), BF16),
            pltpu.VMEM((vals, width), BF16),
            pltpu.VMEM((width, 2 * nz * toks), BF16),
            pltpu.VMEM((2 * nz * toks, span), BF16),
            pltpu.VMEM((nz, 2, vals, toks), F32),
            pltpu.VMEM((toks, D), BF16),
            pltpu.VMEM((2, nz, 2, rows_v, toks), F32),
            pltpu.VMEM((planes, nz, 2, rows_v, toks), F32),
            pltpu.VMEM((2, 8, LANES), F32),
            pltpu.VMEM((nx, 8, LANES), F32),
            pltpu.VMEM((nz, 8, LANES), F32),
            sem(nz, hp), sem(nz, hp), sem(nz, hp), sem(nz, hp), sem(nz, hp),
            sem(nz, vp), sem(nz, vp), sem(nz, vp), sem(nz, vp), sem(nz, vp),
            sem(2 * nz - 1), sem(2 * nz - 1), sem(max(nx - 1, 1)), sem(max(nx - 1, 1)),
            sem(2, 2 * nz - 1), sem(nz, 2), sem(max(nx - 1, 1)), sem(max(nx - 1, 1)),
            sem(1), sem(1), sem(max(nx - 1, 1)), sem(max(nx - 1, 1)),
            sem(1), sem(1), sem(max(nx - 1, 1)), sem(max(nx - 1, 1)), sem(nz - 1), sem(nz - 1),
        ],
        compiler_params=pltpu.CompilerParams(
            collective_id=0, has_side_effects=True, vmem_limit_bytes=56 * 1024 * 1024
        ),
        cost_estimate=pl.CostEstimate(flops=4500000000, bytes_accessed=20000000, transcendentals=0),
    )(val_hidden, val_cotan, val_count, train_hidden, train_cotan, seq_len, seq_device)
    return out, weight.reshape(seqs)


def solution(mesh):
    return jax.shard_map(
        functools.partial(shards, mesh.shape["dp"], mesh.shape["tensor"]),
        mesh=mesh,
        in_specs=(
            P(("groups", "dp", "sub"), "tensor"),
            P(("groups", "dp", "sub"), None),
            P(("groups", "dp", "sub")),
            P(("groups", "dp", "sub"), "tensor"),
            P(("groups", "dp", "sub"), None),
            P("groups"),
            P("groups"),
        ),
        out_specs=(P(("groups", "tensor"), ("dp", "sub")), P("groups")),
        check_vma=False,
    )
```
